32 devices in a mesh: dp: 4 (over y, x), gz: 8 (over z, core).
Axes of the slice: x: 2, y: 2, z: 4, core: 2. Of those that a mesh axis runs over, the one named last changes fastest.
Arguments:
- fields: bfloat16 [4, 64, 16, 128, 128], P('dp', 'gz'), may hold values from -6 to 6
- cotangent: bfloat16 [4, 64, 16, 128, 128], P('dp', 'gz'), may hold values from -6 to 6
- spectral_weight: bfloat16 [2, 16, 16, 32768], P(None, None, None, 'gz'), may hold values from -1.5 to 1.5
- pointwise_weight: bfloat16 [16, 16], replicated, may hold values from -1.5 to 1.5
Outputs:
- layer_output: bfloat16 [4, 64, 16, 128, 128], P('dp', 'gz')
- input_grad: bfloat16 [4, 64, 16, 128, 128], P('dp', 'gz')
- pointwise_grad: float32 [16, 16], replicated
- spectral_grad: float32 [2, 16, 16, 32768], P(None, None, None, 'gz')
The draws below stay inside these ranges and needn't reach their ends.
All inputs are finite; a program needn't handle non-finite values.
Results may differ from the reference program's by a relative error of at most 0.001.
Values sent between devices are 32-bit elements; how exact they have to be, the bound alone decides.
No kernel may reach another device: no remote copies, remote signals or barrier semaphores. Data moves between devices by JAX's collectives and lax.ppermute only.
A program may use at most 128 MiB of HBM per device.

```python
import math
import jax
import jax.numpy as jnp
from jax import lax

C = 16
M = 32
X = 128
Y = 128
Z = 64
SAMPLES = 4
MODES = 32768


def level_of(stream_key, dims, pieces, smallest, high):
    def one(position, blocks):
        steps = jax.random.uniform(jax.random.fold_in(jax.random.fold_in(stream_key, 6), position), (blocks,), jnp.float32, smallest / len(pieces), high / len(pieces))
        return jnp.repeat(jnp.exp(steps), dims[position] // blocks).reshape((-1,) + (1,) * (len(dims) - position - 1))

    loudness = one(*pieces[0])
    for cut in pieces[1:]:
        loudness = loudness * one(*cut)
    return loudness


def bell_draw(own_key, dims, width, reach, shards=(), kind=jnp.bfloat16):
    gain = level_of(own_key, dims, shards, -0.22, 0.18) if shards else 1.0
    drawn = jax.random.normal(own_key, dims, jnp.float32) * width * gain
    return jnp.minimum(jnp.maximum(drawn, -reach), reach).astype(kind)


def setup_inputs(seed: int = 0) -> dict:
    keys = jax.random.split(jax.random.key(seed), 5)
    return {
        "fields": bell_draw(keys[0], (SAMPLES, Z, C, X, Y), 1.0, 6.0, ((0, 4), (1, 8))),
        "cotangent": bell_draw(keys[1], (SAMPLES, Z, C, X, Y), 1.0, 6.0, ((0, 4), (1, 8))),
        "spectral_weight": bell_draw(keys[2], (2, C, C, MODES), C ** -0.5, 1.5, ((3, 8),)),
        "pointwise_weight": bell_draw(keys[3], (C, C), C ** -0.5, 1.5),
    }


HIGHEST = lax.Precision.HIGHEST

def angle_table(length, modes, first, count):
    positions = first + jnp.arange(count, dtype=jnp.int32)
    frequency = jnp.arange(modes, dtype=jnp.int32)
    phase = positions[:, None] * frequency[None, :] % length
    angles = phase.astype(jnp.float32) * (2.0 * math.pi / length)
    return (jnp.cos(angles), jnp.sin(angles))

def plane_forward(field, cos_x, sin_x, cos_y, sin_y):
    modes = cos_x.shape[1]
    section = jnp.einsum('szcxy,yb->szcxb', field, jnp.concatenate([cos_y, -sin_y], axis=1), precision=HIGHEST)
    block = jnp.einsum('szcxb,xa->szcab', section, jnp.concatenate([cos_x, -sin_x], axis=1), precision=HIGHEST)
    real_part = block[..., :modes, :modes] - block[..., modes:, modes:]
    imag_part = block[..., :modes, modes:] + block[..., modes:, :modes]
    shape = real_part.shape[:3] + (modes * modes,)
    return jnp.stack([real_part.reshape(shape), imag_part.reshape(shape)])

def depth_forward(planes, cos_z, sin_z):

    def contract(values, table):
        return jnp.einsum('szcp,zk->scpk', values, table, precision=HIGHEST)
    real_out = contract(planes[0], cos_z) + contract(planes[1], sin_z)
    imag_out = contract(planes[1], cos_z) - contract(planes[0], sin_z)
    shape = real_out.shape[:2] + (real_out.shape[2] * real_out.shape[3],)
    return jnp.stack([real_out.reshape(shape), imag_out.reshape(shape)])

def depth_inverse(spectrum, cos_z, sin_z):
    modes = cos_z.shape[1]
    shape = spectrum.shape[1:3] + (spectrum.shape[3] // modes, modes)
    real_in = spectrum[0].reshape(shape)
    imag_in = spectrum[1].reshape(shape)

    def expand(values, table):
        return jnp.einsum('scpk,zk->szcp', values, table, precision=HIGHEST)
    real_out = expand(real_in, cos_z) - expand(imag_in, sin_z)
    imag_out = expand(real_in, sin_z) + expand(imag_in, cos_z)
    return jnp.stack([real_out, imag_out])

def plane_inverse(planes, cos_x, sin_x, cos_y, sin_y):
    modes = cos_x.shape[1]
    shape = planes.shape[1:4] + (modes, modes)
    real_in = planes[0].reshape(shape)
    imag_in = planes[1].reshape(shape)

    def spread(values, table):
        return jnp.einsum('szcab,xa->szcxb', values, table, precision=HIGHEST)
    real_mid = spread(real_in, cos_x) - spread(imag_in, sin_x)
    imag_mid = spread(real_in, sin_x) + spread(imag_in, cos_x)
    joined = jnp.concatenate([real_mid, imag_mid], axis=-1)
    return jnp.einsum('szcxb,yb->szcxy', joined, jnp.concatenate([cos_y, -sin_y], axis=1), precision=HIGHEST)

def mix_modes(spectrum, weight):

    def term(values, table):
        return jnp.einsum('scm,com->som', values, table, precision=HIGHEST)
    real_out = term(spectrum[0], weight[0]) - term(spectrum[1], weight[1])
    imag_out = term(spectrum[0], weight[1]) + term(spectrum[1], weight[0])
    return jnp.stack([real_out, imag_out])

def mix_adjoint(grad_spec, weight):

    def term(values, table):
        return jnp.einsum('som,com->scm', values, table, precision=HIGHEST)
    real_out = term(grad_spec[0], weight[0]) + term(grad_spec[1], weight[1])
    imag_out = term(grad_spec[1], weight[0]) - term(grad_spec[0], weight[1])
    return jnp.stack([real_out, imag_out])

def mix_weight_grad(spectrum, grad_spec):

    def term(values, other):
        return jnp.einsum('scm,som->com', values, other, precision=HIGHEST)
    real_out = term(spectrum[0], grad_spec[0]) + term(spectrum[1], grad_spec[1])
    imag_out = term(spectrum[0], grad_spec[1]) - term(spectrum[1], grad_spec[0])
    return jnp.stack([real_out, imag_out])

def gelu_tanh(values):
    return jax.nn.gelu(values, approximate=True)

def reference(fields, cotangent, spectral_weight, pointwise_weight):
    cos_x, sin_x = angle_table(X, M, 0, X)
    cos_y, sin_y = angle_table(Y, M, 0, Y)
    cos_z, sin_z = angle_table(Z, M, 0, Z)
    scale = 1.0 / math.sqrt(X * Y * Z * MODES)
    weight = spectral_weight.astype(jnp.float32)
    mixing = pointwise_weight.astype(jnp.float32)

    def one_sample(pair):
        field, cot = pair
        inputs = field.astype(jnp.float32)[None]
        input_spec = depth_forward(plane_forward(inputs, cos_x, sin_x, cos_y, sin_y), cos_z, sin_z)
        mixed = mix_modes(input_spec, weight)
        spectral = plane_inverse(depth_inverse(mixed, cos_z, sin_z), cos_x, sin_x, cos_y, sin_y) * scale
        pointwise = jnp.einsum('szcxy,co->szoxy', inputs, mixing, precision=HIGHEST)
        pre = spectral + pointwise
        activation, pullback = jax.vjp(gelu_tanh, pre)
        grad_pre = pullback(cot.astype(jnp.float32)[None])[0]
        grad_spec = depth_forward(plane_forward(grad_pre, cos_x, sin_x, cos_y, sin_y), cos_z, sin_z) * scale
        adjoint = mix_adjoint(grad_spec, weight)
        back = plane_inverse(depth_inverse(adjoint, cos_z, sin_z), cos_x, sin_x, cos_y, sin_y)
        grad_input = back + jnp.einsum('szoxy,co->szcxy', grad_pre, mixing, precision=HIGHEST)
        point_term = jnp.einsum('szcxy,szoxy->co', inputs, grad_pre, precision=HIGHEST)
        spec_term = mix_weight_grad(input_spec, grad_spec)
        return (activation[0].astype(jnp.bfloat16), grad_input[0].astype(jnp.bfloat16), point_term, spec_term)
    outputs = lax.map(one_sample, (fields, cotangent))
    cells = SAMPLES * X * Y * Z
    pointwise_grad = lax.optimization_barrier(jnp.sum(outputs[2], axis=0)) * (1.0 / math.sqrt(cells))
    spectral_grad = lax.optimization_barrier(jnp.sum(outputs[3], axis=0)) * math.sqrt(MODES / cells)
    return (outputs[0], outputs[1], pointwise_grad, spectral_grad)
```

```python
import functools
import math

import jax
import jax.numpy as jnp
import ml_dtypes
import numpy as np
from jax import lax
from jax.experimental import pallas as pl
from jax.experimental.pallas import tpu as pltpu
from jax.sharding import PartitionSpec as P

M = 32
QUAD = 4
F32 = jnp.float32
BF16 = jnp.bfloat16
NN = (((1,), (0,)), ((), ()))
TN = (((0,), (0,)), ((), ()))
NT = (((1,), (1,)), ((), ()))
GELU_A = math.sqrt(2.0 / math.pi)
GELU_B = 0.044715


def halves(table):
    high = table.astype(np.float32).astype(ml_dtypes.bfloat16)
    low = (table - high.astype(np.float64)).astype(np.float32).astype(ml_dtypes.bfloat16)
    return high, low


def trig(length, modes):
    phase = np.outer(np.arange(length), modes) % length
    angles = phase * (2.0 * math.pi / length)
    return np.cos(angles), np.sin(angles)


def complex_block(cos, sin, sign):
    return np.array([[cos, sign * sin], [-sign * sin, cos]])


def tables(width_x, width_y, depth, owned_x):
    order_y = (np.arange(M) % (M // QUAD)) * QUAD + np.arange(M) // (M // QUAD)
    cos_x, sin_x = trig(width_x, np.arange(M))
    cos_y, sin_y = trig(width_y, order_y)
    cos_z, sin_z = trig(depth, np.arange(M))
    eye4 = np.eye(QUAD)
    eye_a = np.eye(owned_x)
    y_fwd = np.einsum("pq,ryb->pyrqb", eye4, np.array([cos_y, -sin_y]))
    y_fwd = y_fwd.reshape(QUAD * width_y, 2 * QUAD * M)
    y_inv = np.einsum("pq,ryb->rpbqy", eye4, np.array([cos_y, -sin_y]))
    y_inv = y_inv.reshape(2 * QUAD * M, QUAD * width_y)
    x_fwd = np.einsum("ijxa->ajix", complex_block(cos_x, sin_x, -1.0)).reshape(2 * M, 2 * width_x)
    x_inv = np.einsum("ijxa->jxai", complex_block(cos_x, sin_x, 1.0)).reshape(2 * width_x, 2 * M)
    ones = np.ones(QUAD)
    z_fwd = np.einsum("ac,ijzk,r->zaicjrk", eye_a, complex_block(cos_z, sin_z, -1.0), ones)
    z_fwd = z_fwd.reshape(depth * owned_x * 2, owned_x * 2 * QUAD * M)
    z_inv = np.einsum("ac,ijzk,r->zcjairk", eye_a, complex_block(cos_z, sin_z, 1.0), ones)
    z_inv = z_inv.reshape(depth * owned_x * 2, owned_x * 2 * QUAD * M)
    xi_h, xi_l = halves(x_inv)
    x_inv4 = np.concatenate([xi_h, xi_l, xi_h, xi_l], axis=1)
    x_fwd2 = np.concatenate(halves(x_fwd), axis=0)
    return dict(
        y_fwd=np.stack(halves(y_fwd)),
        y_inv=np.stack(halves(y_inv)),
        x_fwd=x_fwd2,
        x_inv=x_inv4,
        z_fwd=np.stack(halves(z_fwd)),
        z_inv=np.stack(halves(z_inv)),
    )


def split(values):
    high = values.astype(BF16)
    return high, (values - high.astype(F32)).astype(BF16)


def dot(left, right, dims=NN):
    return lax.dot_general(left, right, dims, preferred_element_type=F32)


def x_forward(real, imag, x_fwd_ref):
    high, low = split(jnp.concatenate([real, imag], axis=0))
    both = dot(x_fwd_ref[...], high)
    rows = both.shape[0] // 2
    return both[:rows] + both[rows:] + dot(x_fwd_ref[:rows], low)


def store_blocks(out_ref, values):
    groups, rows = out_ref.shape[0], out_ref.shape[2]
    for d in range(groups):
        out_ref[d, 0] = values[d * rows:(d + 1) * rows]


def load_blocks(in_ref, scratch):
    groups, rows = in_ref.shape[0], in_ref.shape[2]
    if rows % 8 == 0:
        return in_ref[:, 0].reshape(groups * rows, in_ref.shape[3])
    for d in range(groups):
        scratch[d * rows:(d + 1) * rows] = in_ref[d, 0]
    return scratch[...]


def fields_kernel(f_ref, y_fwd_ref, x_fwd_ref, out_ref):
    channels = f_ref.shape[2]
    real, imag = [], []
    for j in range(channels // QUAD):
        planes = jnp.concatenate([f_ref[0, 0, QUAD * j + p] for p in range(QUAD)], axis=1)
        g = dot(planes, y_fwd_ref[0]) + dot(planes, y_fwd_ref[1])
        half = g.shape[1] // 2
        real.append(g[:, :half])
        imag.append(g[:, half:])
    values = x_forward(jnp.concatenate(real, axis=1), jnp.concatenate(imag, axis=1), x_fwd_ref)
    store_blocks(out_ref, values)


def inverse_planes(p, x_inv_ref, y_inv_ref):
    high, low = split(p)
    q = dot(x_inv_ref[...], jnp.concatenate([high, high, low, low], axis=0))
    q_high, q_low = split(q)
    rows = q.shape[0] // 2
    wide = QUAD * M
    for j in range(q.shape[1] // wide):
        here = slice(j * wide, (j + 1) * wide)
        left_high = jnp.concatenate([q_high[:rows, here], q_high[rows:, here]], axis=1)
        left_low = jnp.concatenate([q_low[:rows, here], q_low[rows:, here]], axis=1)
        yield j, (
            dot(left_high, y_inv_ref[0]) + dot(left_high, y_inv_ref[1]) + dot(left_low, y_inv_ref[0])
        )


def middle_kernel(p_ref, f_ref, cot_ref, w1_ref, w2_ref, y_fwd_ref, x_fwd_ref, y_inv_ref, x_inv_ref,
                  act_ref, part_ref, out_ref, pg_ref, p_scr, spec, g_high, g_low):
    channels, width_x, width_y = f_ref.shape[2:]
    group = 16

    @pl.when(pl.program_id(0) == 0)
    def _():
        pg_ref[...] = jnp.zeros_like(pg_ref)

    for j, value in inverse_planes(load_blocks(p_ref, p_scr), x_inv_ref, y_inv_ref):
        for p in range(QUAD):
            spec[QUAD * j + p] = value[:, p * width_y:(p + 1) * width_y]

    rows = channels * group

    def step(t, carry):
        first = pl.multiple_of(t * 2 * group, 2 * group)
        cells = [pl.ds(first, group), pl.ds(first + group, group)]

        def both(read):
            return jnp.concatenate([read(s).reshape(rows, width_y) for s in cells], axis=1)

        f = both(lambda s: f_ref[0, 0, :, s, :])
        pre = dot(w1_ref[...], f) + both(lambda s: spec[:, s, :])
        square = pre * pre
        t_val = jnp.tanh(GELU_A * pre * (1.0 + GELU_B * square))
        cdf = 0.5 + 0.5 * t_val
        act = (pre * cdf).astype(BF16)
        slope = cdf + pre * (0.5 - 0.5 * t_val * t_val) * (GELU_A + 3.0 * GELU_A * GELU_B * square)
        g = both(lambda s: cot_ref[0, 0, :, s, :]).astype(F32) * slope
        high, low = split(g)
        part = dot(w2_ref[...], high) + dot(w2_ref[...], low)
        pg = None
        for i, s in enumerate(cells):
            lanes = slice(i * width_y, (i + 1) * width_y)
            shape = (channels, group, width_y)
            act_ref[0, 0, :, s, :] = act[:, lanes].reshape(shape)
            part_ref[0, :, s, :] = part[:, lanes].reshape(shape)
            g_high[:, s, :] = high[:, lanes].reshape(shape)
            g_low[:, s, :] = low[:, lanes].reshape(shape)
        pg_ref[...] += dot(f, high, NT) + dot(f, low, NT)
        return carry

    lax.fori_loop(0, width_x // (2 * group), step, 0)

    real, imag = [], []
    for j in range(channels // QUAD):
        planes = [jnp.concatenate([r[QUAD * j + p] for p in range(QUAD)], axis=1) for r in (g_high, g_low)]
        v = dot(planes[0], y_fwd_ref[0]) + dot(planes[0], y_fwd_ref[1]) + dot(planes[1], y_fwd_ref[0])
        half = v.shape[1] // 2
        real.append(v[:, :half])
        imag.append(v[:, half:])
    values = x_forward(jnp.concatenate(real, axis=1), jnp.concatenate(imag, axis=1), x_fwd_ref)
    store_blocks(out_ref, values)


def final_kernel(p_ref, part_ref, y_inv_ref, x_inv_ref, out_ref, p_scr):
    width_y = out_ref.shape[4]
    for j, value in inverse_planes(load_blocks(p_ref, p_scr), x_inv_ref, y_inv_ref):
        for p in range(QUAD):
            c = QUAD * j + p
            out_ref[0, 0, c] = (value[:, p * width_y:(p + 1) * width_y] + part_ref[0, c]).astype(BF16)


def lane_quad(shape):
    return lax.broadcasted_iota(jnp.int32, shape, len(shape) - 1) // M


def depth_forward(s_ref, z_fwd_ref, spec_ref, scale):
    high, low = split(s_ref[...])
    v = dot(high, z_fwd_ref[0], TN) + dot(high, z_fwd_ref[1], TN) + dot(low, z_fwd_ref[0], TN)
    tall = M // QUAD
    wide = QUAD * M
    channels = v.shape[0] // M
    v = v.reshape(channels, QUAD, tall, v.shape[1])
    quad = lane_quad((channels, tall, wide))
    for a in range(v.shape[3] // (2 * wide)):
        for part in range(2):
            lanes = slice((2 * a + part) * wide, (2 * a + part + 1) * wide)
            u = v[:, 0, :, lanes]
            for r in range(1, QUAD):
                u = jnp.where(quad == r, v[:, r, :, lanes], u)
            spec_ref[part, :, a * tall:(a + 1) * tall, :] = u * scale if scale != 1.0 else u


def depth_inverse(spec_ref, z_inv_ref, out_ref):
    channels, places, wide = spec_ref.shape[1:]
    tall = M // QUAD
    quad = lane_quad((channels, tall, wide))
    pieces = []
    for a in range(places // tall):
        for part in range(2):
            v = spec_ref[part, :, a * tall:(a + 1) * tall, :]
            masked = jnp.stack([jnp.where(quad == r, v, 0.0) for r in range(QUAD)], axis=1)
            pieces.append(masked.reshape(channels * M, wide))
    high, low = split(jnp.concatenate(pieces, axis=1))
    out_ref[...] = dot(z_inv_ref[0], high, NT) + dot(z_inv_ref[1], high, NT) + dot(z_inv_ref[0], low, NT)


def mix_kernel(scale, s_ref, r_ref, z_fwd_ref, z_inv_ref, out_ref, u_ref, v_scr):
    channels, places, wide = u_ref.shape[1:]
    depth_forward(s_ref, z_fwd_ref, u_ref, 1.0)

    def step(q, carry):
        lanes = pl.ds(pl.multiple_of(q * wide, wide), wide)
        real = jnp.zeros((channels, wide), F32)
        imag = jnp.zeros((channels, wide), F32)
        for c in range(channels):
            w_re = r_ref[0, c, :, lanes].astype(F32)
            w_im = r_ref[1, c, :, lanes].astype(F32)
            u_re = u_ref[0, c, pl.ds(q, 1), :]
            u_im = u_ref[1, c, pl.ds(q, 1), :]
            real += u_re * w_re - u_im * w_im
            imag += u_re * w_im + u_im * w_re
        v_scr[0, :, pl.ds(q, 1), :] = (real * scale)[:, None, :]
        v_scr[1, :, pl.ds(q, 1), :] = (imag * scale)[:, None, :]
        return carry

    lax.fori_loop(0, places, step, 0)
    depth_inverse(v_scr, z_inv_ref, out_ref)


def adjoint_kernel(scale, s_ref, r_ref, z_fwd_ref, z_inv_ref, out_ref, dv_ref, du_scr):
    channels, places, wide = dv_ref.shape[1:]
    depth_forward(s_ref, z_fwd_ref, dv_ref, scale)

    def step(q, carry):
        lanes = pl.ds(pl.multiple_of(q * wide, wide), wide)
        d_re = dv_ref[0, :, pl.ds(q, 1), :].reshape(channels, wide)
        d_im = dv_ref[1, :, pl.ds(q, 1), :].reshape(channels, wide)
        for c in range(channels):
            w_re = r_ref[0, c, :, lanes].astype(F32)
            w_im = r_ref[1, c, :, lanes].astype(F32)
            du_scr[0, c, pl.ds(q, 1), :] = jnp.sum(d_re * w_re + d_im * w_im, axis=0, keepdims=True)
            du_scr[1, c, pl.ds(q, 1), :] = jnp.sum(d_im * w_re - d_re * w_im, axis=0, keepdims=True)
        return carry

    lax.fori_loop(0, places, step, 0)
    depth_inverse(du_scr, z_inv_ref, out_ref)


def weight_grad_kernel(scale, *refs):
    count = (len(refs) - 1) // 2
    u_refs, dv_refs, out_ref = refs[:count], refs[count:2 * count], refs[-1]
    channels, places, wide = u_refs[0].shape[1:]
    for q in range(places):
        lanes = slice(q * wide, (q + 1) * wide)
        dv = [[r[part, :, q, :] * scale for part in range(2)] for r in dv_refs]
        for c in range(channels):
            real = imag = None
            for s in range(count):
                u_re = u_refs[s][0, c, q:q + 1, :]
                u_im = u_refs[s][1, c, q:q + 1, :]
                d_re, d_im = dv[s]
                t_re = u_re * d_re + u_im * d_im
                t_im = u_re * d_im - u_im * d_re
                real = t_re if real is None else real + t_re
                imag = t_im if imag is None else imag + t_im
            out_ref[0, c, :, lanes] = real
            out_ref[1, c, :, lanes] = imag


def params(steps, megabytes=48):
    return pltpu.CompilerParams(
        dimension_semantics=("arbitrary",) * steps, vmem_limit_bytes=megabytes * 1024 * 1024
    )


def whole_spec(array):
    rank = len(array.shape)
    return pl.BlockSpec(tuple(array.shape), lambda *i: (0,) * rank)


def shards(fields, cotangent, spectral_weight, pointwise_weight):
    groups = lax.axis_size("gz")
    samples = lax.axis_size("dp")
    _, near, channels, width_x, width_y = fields.shape
    depth = near * groups
    owned = M // groups
    rows = 2 * owned
    wide = channels * M
    places = spectral_weight.shape[3] // (QUAD * M)
    total_modes = M * M * M
    cells = samples * width_x * width_y * depth
    scale = 1.0 / math.sqrt(width_x * width_y * depth * total_modes)
    tab = {k: jnp.asarray(v) for k, v in tables(width_x, width_y, depth, owned).items()}

    plane = pl.BlockSpec((1, 1, channels, width_x, width_y), lambda z: (0, z, 0, 0, 0))
    part_spec = pl.BlockSpec((1, channels, width_x, width_y), lambda z: (z, 0, 0, 0))
    block = pl.BlockSpec((groups, 1, rows, wide), lambda z: (0, z, 0, 0))
    block_shape = jax.ShapeDtypeStruct((groups, near, rows, wide), F32)
    spec_shape = jax.ShapeDtypeStruct((2, channels, places, QUAD * M), F32)
    out_field = jax.ShapeDtypeStruct(fields.shape, BF16)
    flat = (depth * rows, wide)

    def exchange(values):
        return lax.all_to_all(values, "gz", 0, 0, tiled=True)

    def gather(values):
        pieces = [values]
        for k in range(1, samples):
            pieces.append(lax.ppermute(values, "dp", [(i, i ^ k) for i in range(samples)]))
        return pieces

    forward = pl.pallas_call(
        fields_kernel,
        grid=(near,),
        in_specs=[plane, whole_spec(tab["y_fwd"]), whole_spec(tab["x_fwd"])],
        out_specs=block,
        out_shape=block_shape,
        compiler_params=params(1),
        name="fields_forward",
    )(fields, tab["y_fwd"], tab["x_fwd"])
    arrived = exchange(forward).reshape(flat)

    mixed, u_spec = pl.pallas_call(
        functools.partial(mix_kernel, scale),
        out_shape=(jax.ShapeDtypeStruct(flat, F32), spec_shape),
        scratch_shapes=[pltpu.VMEM(spec_shape.shape, F32)],
        compiler_params=params(0),
        name="mix_modes",
    )(arrived, spectral_weight, tab["z_fwd"], tab["z_inv"])
    u_all = gather(u_spec)
    planes = exchange(mixed.reshape(block_shape.shape))

    eye = jnp.eye(16, dtype=BF16)
    weight1 = jnp.kron(pointwise_weight.T, eye)
    weight2 = jnp.kron(pointwise_weight, eye)
    side = channels * 16
    scratch_planes = (channels, width_x, width_y)
    layer_output, part, grad_forward, point = pl.pallas_call(
        middle_kernel,
        grid=(near,),
        in_specs=[block, plane, plane, whole_spec(weight1), whole_spec(weight2), whole_spec(tab["y_fwd"]),
                  whole_spec(tab["x_fwd"]), whole_spec(tab["y_inv"]), whole_spec(tab["x_inv"])],
        out_specs=[plane, part_spec, block, pl.BlockSpec((side, side), lambda z: (0, 0))],
        out_shape=[out_field, jax.ShapeDtypeStruct((near, *scratch_planes), F32), block_shape,
                   jax.ShapeDtypeStruct((side, side), F32)],
        scratch_shapes=[pltpu.VMEM((2 * M, wide), F32), pltpu.VMEM(scratch_planes, F32),
                        pltpu.VMEM(scratch_planes, BF16), pltpu.VMEM(scratch_planes, BF16)],
        compiler_params=params(1),
        name="middle",
    )(planes, fields, cotangent, weight1, weight2, tab["y_fwd"], tab["x_fwd"], tab["y_inv"], tab["x_inv"])

    arrived = exchange(grad_forward).reshape(flat)
    adjoint, dv_spec = pl.pallas_call(
        functools.partial(adjoint_kernel, scale),
        out_shape=(jax.ShapeDtypeStruct(flat, F32), spec_shape),
        scratch_shapes=[pltpu.VMEM(spec_shape.shape, F32)],
        compiler_params=params(0),
        name="mix_adjoint",
    )(arrived, spectral_weight, tab["z_fwd"], tab["z_inv"])
    dv_all = gather(dv_spec)
    planes = exchange(adjoint.reshape(block_shape.shape))

    input_grad = pl.pallas_call(
        final_kernel,
        grid=(near,),
        in_specs=[block, part_spec, whole_spec(tab["y_inv"]), whole_spec(tab["x_inv"])],
        out_specs=plane,
        out_shape=out_field,
        scratch_shapes=[pltpu.VMEM((2 * M, wide), F32)],
        compiler_params=params(1),
        name="input_gradient",
    )(planes, part, tab["y_inv"], tab["x_inv"])

    tall = 8
    spec_block = pl.BlockSpec((2, channels, tall, QUAD * M), lambda q: (0, 0, q, 0))
    spectral_grad = pl.pallas_call(
        functools.partial(weight_grad_kernel, math.sqrt(total_modes / cells)),
        grid=(places // tall,),
        in_specs=[spec_block] * (2 * samples),
        out_specs=pl.BlockSpec((2, channels, channels, tall * QUAD * M), lambda q: (0, 0, 0, q)),
        out_shape=jax.ShapeDtypeStruct(spectral_weight.shape, F32),
        compiler_params=params(1),
        name="weight_gradient",
    )(*u_all, *dv_all)

    point = jnp.einsum("cxox->co", point.reshape(channels, 16, channels, 16))
    pointwise_grad = lax.psum(point, ("dp", "gz")) * (1.0 / math.sqrt(cells))
    return layer_output, input_grad, pointwise_grad, spectral_grad


def solution(mesh):
    placed = (
        P("dp", "gz", None, None, None),
        P("dp", "gz", None, None, None),
        P(None, None, None, "gz"),
        P(),
    )
    return jax.shard_map(
        shards,
        mesh=mesh,
        in_specs=placed,
        out_specs=(
            P("dp", "gz", None, None, None),
            P("dp", "gz", None, None, None),
            P(),
            P(None, None, None, "gz"),
        ),
        check_vma=False,
    )
```

```python
import functools
import math

import jax
import jax.numpy as jnp
import ml_dtypes
import numpy as np
from jax import lax
from jax.experimental import pallas as pl
from jax.experimental.pallas import tpu as pltpu
from jax.sharding import PartitionSpec as P

M = 32
QUAD = 4
CORES = 2
GROUP = 16
F32 = jnp.float32
BF16 = jnp.bfloat16
NN = (((1,), (0,)), ((), ()))
TN = (((0,), (0,)), ((), ()))
NT = (((1,), (1,)), ((), ()))
GELU_A = math.sqrt(2.0 / math.pi)
GELU_B = 0.044715


def halves(table):
    high = table.astype(np.float32).astype(ml_dtypes.bfloat16)
    low = (table - high.astype(np.float64)).astype(np.float32).astype(ml_dtypes.bfloat16)
    return high, low


def thrice(table):
    high, low = halves(table)
    return np.concatenate([high, low, high])


def trig(length, modes):
    phase = np.outer(np.arange(length), modes) % length
    angles = phase * (2.0 * math.pi / length)
    return np.cos(angles), np.sin(angles)


def complex_block(cos, sin, sign):
    return np.array([[cos, sign * sin], [-sign * sin, cos]])


def tables(width_x, width_y, depth, owned_x):
    order_y = (np.arange(M) % (M // QUAD)) * QUAD + np.arange(M) // (M // QUAD)
    cos_x, sin_x = trig(width_x, np.arange(M))
    cos_y, sin_y = trig(width_y, order_y)
    cos_z, sin_z = trig(depth, np.arange(M))
    eye4 = np.eye(QUAD)
    eye_a = np.eye(owned_x)
    y_fwd = np.einsum("pq,ryb->pyrqb", eye4, np.array([cos_y, -sin_y]))
    y_fwd = y_fwd.reshape(QUAD * width_y, 2 * QUAD * M)
    y_inv = np.einsum("pq,ryb->rpbqy", eye4, np.array([cos_y, -sin_y]))
    y_inv = y_inv.reshape(2 * QUAD * M, QUAD * width_y)
    x_fwd = np.einsum("ijxa->ajix", complex_block(cos_x, sin_x, -1.0)).reshape(2 * M, 2 * width_x)
    x_inv = np.einsum("ijxa->jxai", complex_block(cos_x, sin_x, 1.0)).reshape(2 * width_x, 2 * M)
    ones = np.ones(QUAD)
    z_fwd = np.einsum("ac,ijzk,r->zaicjrk", eye_a, complex_block(cos_z, sin_z, -1.0), ones)
    z_fwd = z_fwd.reshape(depth * owned_x * 2, owned_x * 2 * QUAD * M)
    z_inv = np.einsum("ac,ijzk,r->zcjairk", eye_a, complex_block(cos_z, sin_z, 1.0), ones)
    z_inv = z_inv.reshape(depth * owned_x * 2, owned_x * 2 * QUAD * M)
    xi_h, xi_l = halves(x_inv)
    x_inv4 = np.concatenate([xi_h, xi_l, xi_h, xi_l], axis=1)
    x_fwd2 = np.concatenate(halves(x_fwd), axis=0)
    return dict(
        y_fwd=thrice(y_fwd),
        y_inv=thrice(y_inv),
        x_fwd=x_fwd2,
        x_inv=x_inv4,
        z_fwd=np.stack(halves(z_fwd)),
        z_inv=np.stack(halves(z_inv)),
    )


def split(values):
    high = values.astype(BF16)
    return high, (values - high.astype(F32)).astype(BF16)


def dot(left, right, dims=NN):
    return lax.dot_general(left, right, dims, preferred_element_type=F32)


def x_forward(real, imag, x_fwd_ref):
    high, low = split(jnp.concatenate([real, imag], axis=0))
    both = dot(x_fwd_ref[...], high)
    rows = both.shape[0] // 2
    return both[:rows] + both[rows:] + dot(x_fwd_ref[:rows], low)


def slot(j, h, chips, first):
    c, k = j // CORES, j % CORES
    base = sum(chips + f for f in first[:h])
    if not first[h]:
        return base + c, k
    return (base + c, 0) if k == 0 else (base + chips, c)


def store_blocks(out_refs, scratch, values, me, t):
    groups, rows = scratch.shape[:2]
    for d in range(groups):
        scratch[d] = values[d * rows:(d + 1) * rows]
    for j in range(groups):
        i, lead = slot(j, 0, groups // CORES, (False,))
        out_refs[i][lead, t] = scratch[me ^ j]


def load_blocks(in_refs, scratch, flat, me, t):
    groups, rows = scratch.shape[:2]
    for j, ref in enumerate(in_refs):
        scratch[me ^ j] = ref[0, t]
    if rows % 8 == 0:
        return scratch[...].reshape(groups * rows, scratch.shape[2])
    for d in range(groups):
        flat[d * rows:(d + 1) * rows] = scratch[d]
    return flat[...]


def fields_kernel(f_ref, y_fwd_ref, x_fwd_ref, *refs):
    out_refs, v_scr = refs[:-1], refs[-1]
    channels = f_ref.shape[2]
    for t in range(f_ref.shape[1]):
        real, imag = [], []
        for j in range(channels // QUAD):
            planes = [f_ref[0, t, QUAD * j + p] for p in range(QUAD)]
            g = dot(jnp.concatenate(planes + planes, axis=1), y_fwd_ref[:2 * QUAD * f_ref.shape[4]])
            half = g.shape[1] // 2
            real.append(g[:, :half])
            imag.append(g[:, half:])
        values = x_forward(jnp.concatenate(real, axis=1), jnp.concatenate(imag, axis=1), x_fwd_ref)
        store_blocks(out_refs, v_scr.at[t], values, lax.axis_index("gz"), t)


def inverse_planes(p, x_inv_ref, y_inv_ref):
    high, low = split(p)
    q = dot(x_inv_ref[...], jnp.concatenate([high, high, low, low], axis=0))
    q_high, q_low = split(q)
    rows = q.shape[0] // 2
    wide = QUAD * M
    for j in range(q.shape[1] // wide):
        here = slice(j * wide, (j + 1) * wide)
        high = [q_high[:rows, here], q_high[rows:, here]]
        low = [q_low[:rows, here], q_low[rows:, here]]
        yield j, dot(jnp.concatenate(high + high + low, axis=1), y_inv_ref[...])


def middle_kernel(groups, *refs):
    in_refs, inputs, (act_ref, part_ref, pg_ref), out_refs, scratch = cut(
        refs, groups, 8, 3, groups // CORES, 8)
    f_ref, cot_ref, w_ref, spread_ref, y_fwd_ref, x_fwd_ref, y_inv_ref, x_inv_ref = inputs
    p_scr, flat, spec, g_high, g_low, w1_ref, w2_ref, pg_scr = scratch
    me = lax.axis_index("gz")
    channels, width_x, width_y = f_ref.shape[2:]
    group = GROUP
    side = channels * group
    same = (lax.broadcasted_iota(jnp.int32, (side, side), 0) % group
            == lax.broadcasted_iota(jnp.int32, (side, side), 1) % group)

    @pl.when(pl.program_id(0) == 0)
    def _():
        pg_scr[...] = jnp.zeros_like(pg_scr)
        spread = spread_ref[...]
        for ref, dims in ((w1_ref, NT), (w2_ref, NN)):
            rows = dot(spread, w_ref[...], dims).astype(BF16)
            ref[...] = jnp.where(same, dot(rows, spread, NT), 0.0).astype(BF16)

    for t in range(f_ref.shape[1]):
        for j, value in inverse_planes(load_blocks(in_refs, p_scr.at[t], flat.at[t], me, t), x_inv_ref, y_inv_ref):
            for p in range(QUAD):
                spec[t, QUAD * j + p] = value[:, p * width_y:(p + 1) * width_y]

        rows = channels * group

        def step(u, carry):
            first = pl.multiple_of(u * 2 * group, 2 * group)
            cells = [pl.ds(first, group), pl.ds(first + group, group)]

            def both(read):
                return jnp.concatenate([read(s).reshape(rows, width_y) for s in cells], axis=1)

            f = both(lambda s: f_ref[0, t, :, s, :])
            pre = dot(w1_ref[...], f) + both(lambda s: spec[t, :, s, :])
            square = pre * pre
            t_val = jnp.tanh(GELU_A * pre * (1.0 + GELU_B * square))
            cdf = 0.5 + 0.5 * t_val
            act = (pre * cdf).astype(BF16)
            slope = cdf + pre * (0.5 - 0.5 * t_val * t_val) * (GELU_A + 3.0 * GELU_A * GELU_B * square)
            g = both(lambda s: cot_ref[0, t, :, s, :]).astype(F32) * slope
            high, low = split(g)
            part = dot(w2_ref[...], high) + dot(w2_ref[...], low)
            pg = None
            for i, s in enumerate(cells):
                lanes = slice(i * width_y, (i + 1) * width_y)
                shape = (channels, group, width_y)
                act_ref[0, t, :, s, :] = act[:, lanes].reshape(shape)
                part_ref[t, :, s, :] = part[:, lanes].reshape(shape)
                g_high[t, :, s, :] = high[:, lanes].reshape(shape)
                g_low[t, :, s, :] = low[:, lanes].reshape(shape)
            pg_scr[...] += dot(f, high, NT) + dot(f, low, NT)
            return carry

        lax.fori_loop(0, width_x // (2 * group), step, 0, unroll=True)

        real, imag = [], []
        for j in range(channels // QUAD):
            high, low = [[r[t, QUAD * j + p] for p in range(QUAD)] for r in (g_high, g_low)]
            v = dot(jnp.concatenate(high + high + low, axis=1), y_fwd_ref[...])
            half = v.shape[1] // 2
            real.append(v[:, :half])
            imag.append(v[:, half:])
        values = x_forward(jnp.concatenate(real, axis=1), jnp.concatenate(imag, axis=1), x_fwd_ref)
        store_blocks(out_refs, p_scr.at[t], values, me, t)

    @pl.when(pl.program_id(0) == pl.num_programs(0) - 1)
    def _():
        spread = spread_ref[...].astype(F32)
        kept = jnp.where(same, pg_scr[...], 0.0)
        right = lax.dot_general(kept, spread, NN, precision=lax.Precision.HIGHEST, preferred_element_type=F32)
        pg_ref[...] = lax.dot_general(spread, right, TN, precision=lax.Precision.HIGHEST, preferred_element_type=F32)


def final_kernel(groups, *refs):
    in_refs, (part_ref, y_inv_ref, x_inv_ref, out_ref, p_scr, flat) = cut(refs, groups, 6)
    me = lax.axis_index("gz")
    width_y = out_ref.shape[4]
    for t in range(out_ref.shape[1]):
        for j, value in inverse_planes(load_blocks(in_refs, p_scr.at[t], flat.at[t], me, t), x_inv_ref, y_inv_ref):
            for p in range(QUAD):
                c = QUAD * j + p
                out_ref[0, t, c] = (value[:, p * width_y:(p + 1) * width_y] + part_ref[t, c]).astype(BF16)


def lane_quad(shape):
    return lax.broadcasted_iota(jnp.int32, shape, len(shape) - 1) // M


def depth_forward(in_refs, s_scr, z_fwd_ref, spec_ref, scale):
    me = lax.axis_index("gz")
    groups = s_scr.shape[0]
    tall = s_scr.shape[1] * groups // len(in_refs)
    for i, ref in enumerate(in_refs):
        h, j = i // groups, i % groups
        s_scr[me ^ j, h * tall:(h + 1) * tall] = ref[0]
    high, low = split(s_scr[...].reshape(-1, s_scr.shape[2]))
    v = dot(high, z_fwd_ref[0], TN) + dot(high, z_fwd_ref[1], TN) + dot(low, z_fwd_ref[0], TN)
    tall = M // QUAD
    wide = QUAD * M
    channels = v.shape[0] // M
    v = v.reshape(channels, QUAD, tall, v.shape[1])
    quad = lane_quad((channels, tall, wide))
    for a in range(v.shape[3] // (2 * wide)):
        for part in range(2):
            lanes = slice((2 * a + part) * wide, (2 * a + part + 1) * wide)
            u = v[:, 0, :, lanes]
            for r in range(1, QUAD):
                u = jnp.where(quad == r, v[:, r, :, lanes], u)
            spec_ref[part, :channels, a * tall:(a + 1) * tall, :] = u * scale if scale != 1.0 else u


def depth_inverse(spec_ref, z_inv_ref, s_scr, out_refs, first):
    channels, places, wide = spec_ref.shape[1:]
    tall = M // QUAD
    quad = lane_quad((channels, tall, wide))
    pieces = []
    for a in range(places // tall):
        for part in range(2):
            v = spec_ref[part, :, a * tall:(a + 1) * tall, :]
            masked = jnp.stack([jnp.where(quad == r, v, 0.0) for r in range(QUAD)], axis=1)
            pieces.append(masked.reshape(channels * M, wide))
    high, low = split(jnp.concatenate(pieces, axis=1))
    values = dot(z_inv_ref[0], high, NT) + dot(z_inv_ref[1], high, NT) + dot(z_inv_ref[0], low, NT)
    s_scr[...] = values.reshape(s_scr.shape)
    me = lax.axis_index("gz")
    groups = s_scr.shape[0]
    tall = s_scr.shape[1] // len(first)
    for h in range(len(first)):
        for j in range(groups):
            i, lead = slot(j, h, groups // CORES, first)
            out_refs[i][lead] = s_scr[me ^ j, h * tall:(h + 1) * tall]


def cut(refs, *counts):
    pieces = []
    for n in counts:
        pieces.append(refs[:n])
        refs = refs[n:]
    return pieces


def mix_kernel(count_in, count_out, first, scale, *refs):
    in_refs, (r_ref, z_fwd_ref, z_inv_ref, u_ref), out_refs, (v_scr, s_scr) = cut(refs, count_in, 4, count_out, 2)
    channels, places, wide = u_ref.shape[1:]
    depth_forward(in_refs, s_scr, z_fwd_ref, u_ref, 1.0)

    def step(q, carry):
        lanes = pl.ds(pl.multiple_of(q * wide, wide), wide)
        real = jnp.zeros((channels, wide), F32)
        imag = jnp.zeros((channels, wide), F32)
        for c in range(channels):
            w_re = r_ref[0, c, :, lanes].astype(F32)
            w_im = r_ref[1, c, :, lanes].astype(F32)
            u_re = u_ref[0, c, pl.ds(q, 1), :]
            u_im = u_ref[1, c, pl.ds(q, 1), :]
            real += u_re * w_re - u_im * w_im
            imag += u_re * w_im + u_im * w_re
        v_scr[0, :, pl.ds(q, 1), :] = (real * scale)[:, None, :]
        v_scr[1, :, pl.ds(q, 1), :] = (imag * scale)[:, None, :]
        return carry

    lax.fori_loop(0, places, step, 0)
    depth_inverse(v_scr, z_inv_ref, s_scr, out_refs, first)


def adjoint_kernel(count_in, count_out, first, scale, *refs):
    in_refs, (point_ref, r_ref, z_fwd_ref, z_inv_ref, dv_ref), out_refs, (du_scr, s_scr) = cut(
        refs, count_in, 5, count_out, 2)
    channels, places, wide = du_scr.shape[1:]
    dv_ref[:, channels:] = jnp.zeros((2, 1, places, wide), F32)
    dv_ref[0, channels, 0:point_ref.shape[0]] = point_ref[...]
    depth_forward(in_refs, s_scr, z_fwd_ref, dv_ref, scale)

    def step(q, carry):
        lanes = pl.ds(pl.multiple_of(q * wide, wide), wide)
        d_re = dv_ref[0, :channels, pl.ds(q, 1), :].reshape(channels, wide)
        d_im = dv_ref[1, :channels, pl.ds(q, 1), :].reshape(channels, wide)
        for c in range(channels):
            w_re = r_ref[0, c, :, lanes].astype(F32)
            w_im = r_ref[1, c, :, lanes].astype(F32)
            du_scr[0, c, pl.ds(q, 1), :] = jnp.sum(d_re * w_re + d_im * w_im, axis=0, keepdims=True)
            du_scr[1, c, pl.ds(q, 1), :] = jnp.sum(d_im * w_re - d_re * w_im, axis=0, keepdims=True)
        return carry

    lax.fori_loop(0, places, step, 0)
    depth_inverse(du_scr, z_inv_ref, s_scr, out_refs, first)


def weight_grad_kernel(scale, *refs):
    u_ref, dv_refs, out_ref = refs[0], refs[1:-1], refs[-1]
    count = len(dv_refs)
    me = lax.axis_index("dp")
    channels, places, wide = u_ref.shape[2:]
    for q in range(places):
        lanes = slice(q * wide, (q + 1) * wide)
        dv = [[r[part, :channels, q, :] * scale for part in range(2)] for r in dv_refs]
        for c in range(channels):
            real = imag = None
            for s in range(count):
                u_re = u_ref[me ^ s, 0, c, q:q + 1, :]
                u_im = u_ref[me ^ s, 1, c, q:q + 1, :]
                d_re, d_im = dv[s]
                t_re = u_re * d_re + u_im * d_im
                t_im = u_re * d_im - u_im * d_re
                real = t_re if real is None else real + t_re
                imag = t_im if imag is None else imag + t_im
            out_ref[0, c, :, lanes] = real
            out_ref[1, c, :, lanes] = imag


def params(steps, megabytes=60):
    return pltpu.CompilerParams(
        dimension_semantics=("arbitrary",) * steps, vmem_limit_bytes=megabytes * 1024 * 1024
    )


def cost(micros):
    return pl.CostEstimate(flops=int(micros * 1.1e9), bytes_accessed=int(micros * 3.5e6), transcendentals=0)


def whole_spec(array):
    rank = len(array.shape)
    return pl.BlockSpec(tuple(array.shape), lambda *i: (0,) * rank)


def shards(fields, cotangent, spectral_weight, pointwise_weight):
    groups = lax.axis_size("gz")
    samples = lax.axis_size("dp")
    _, near, channels, width_x, width_y = fields.shape
    depth = near * groups
    owned = M // groups
    rows = 2 * owned
    wide = channels * M
    places = spectral_weight.shape[3] // (QUAD * M)
    total_modes = M * M * M
    cells = samples * width_x * width_y * depth
    scale = 1.0 / math.sqrt(width_x * width_y * depth * total_modes)
    tab = {k: jnp.asarray(v) for k, v in tables(width_x, width_y, depth, owned).items()}

    chips = groups // CORES
    cut_out = 2
    part_near = near // cut_out
    batch = 2
    plane_shape = (1, batch, channels, width_x, width_y)
    plane = pl.BlockSpec(plane_shape, lambda z: (0, z, 0, 0, 0))

    def block(planes):
        return pl.BlockSpec((CORES, planes, rows, wide), lambda z: (0, z, 0, 0))

    def scratch(planes):
        return [pltpu.VMEM((planes, groups, rows, wide), F32),
                pltpu.VMEM((planes, groups * rows if rows % 8 else 8, wide), F32)]

    spec_shape = jax.ShapeDtypeStruct((2, channels, places, QUAD * M), F32)

    def sent(planes):
        return [jax.ShapeDtypeStruct((CORES, planes, rows, wide), F32)] * chips

    def hop(values, j):
        return lax.ppermute(values, "gz", [(i, i ^ j) for i in range(groups)])

    far_first = sorted(range(1, chips), key=lambda c: (-(c & (chips // 2)), c))

    def cross(blocks):
        got = [blocks[0]] + [None] * (chips - 1)
        for c in far_first:
            got[c] = hop(blocks[c], CORES * c)
        return got

    def swap(got):
        swapped = hop(jnp.stack([g[1] for g in got]), 1)
        return [(got[j // CORES], 0) if j % CORES == 0 else (swapped, j // CORES) for j in range(groups)]

    def swap_last(blocks):
        return swap(cross(blocks))

    def swap_first(blocks):
        *near_blocks, crossing = blocks
        swapped = hop(crossing, 1)
        got = [None] * chips
        for c in far_first:
            got[c] = hop(jnp.concatenate([near_blocks[c], swapped[c:c + 1]]), CORES * c)
        return [(near_blocks[0], 0), (swapped, 0)] + [(got[j // CORES], j % CORES) for j in range(CORES, groups)]

    def reshaped(arrays, *shape):
        return [v.reshape(v.shape[0], *shape) for v in arrays]

    def gather(values):
        pieces = [values]
        for k in range(1, samples):
            pieces.append(lax.ppermute(values, "dp", [(i, i ^ k) for i in range(samples)]))
        return pieces

    def plane_specs(arrived, planes):
        def one(lead):
            return pl.BlockSpec((1, planes, rows, wide), lambda z: (lead, z, 0, 0))
        return [v for v, _ in arrived], [one(lead) for _, lead in arrived]

    def mix_call(kernel, name, arrived, first, factor, *extra):
        pieces = [p for half in arrived for p in half]
        tall = near // len(arrived) * rows
        operands = [v.reshape(v.shape[0], tall, wide) for v, _ in pieces]

        def one(lead):
            return pl.BlockSpec((1, tall, wide), lambda i: (lead, 0, 0))

        constants = [*extra, spectral_weight, tab["z_fwd"], tab["z_inv"]]
        made = jax.ShapeDtypeStruct((2, channels + len(extra), places, QUAD * M), F32)
        halves = len(first)
        low = near // halves * rows
        outs = []
        for f in first:
            outs += [jax.ShapeDtypeStruct((1 if f else CORES, low, wide), F32)] * chips
            outs += [jax.ShapeDtypeStruct((chips, low, wide), F32)] * f
        result = pl.pallas_call(
            functools.partial(kernel, len(operands), len(outs), first, factor),
            grid=(1,),
            in_specs=[one(lead) for _, lead in pieces] + [whole_spec(v) for v in constants],
            out_specs=[whole_spec(made)] + [whole_spec(v) for v in outs],
            out_shape=[made] + outs,
            scratch_shapes=[pltpu.VMEM(spec_shape.shape, F32), pltpu.VMEM((groups, near * rows, wide), F32)],
            compiler_params=params(1),
            name=name,
            cost_estimate=cost(9),
        )(*operands, *constants)
        blocks = reshaped(result[1:], near // halves, rows, wide)
        return result[0], cut(blocks, *[chips + f for f in first])

    forward = pl.pallas_call(
        fields_kernel,
        grid=(near // batch,),
        in_specs=[plane, whole_spec(tab["y_fwd"]), whole_spec(tab["x_fwd"])],
        out_specs=[block(batch)] * chips,
        out_shape=sent(near),
        scratch_shapes=scratch(batch)[:1],
        compiler_params=params(1),
        name="fields_forward",
        cost_estimate=cost(5),
    )(fields, tab["y_fwd"], tab["x_fwd"])
    arrived = [swap_last(forward)]

    u_spec, mixed = mix_call(mix_kernel, "mix_modes", arrived, (False, True), scale)
    planes = [swap_last(mixed[0]), swap_first(mixed[1])]
    u_all = lax.all_gather(u_spec, "dp")

    side = channels * GROUP
    spread = jnp.asarray(np.kron(np.eye(channels), np.ones((GROUP, 1))).astype(ml_dtypes.bfloat16))
    scratch_planes = (channels, width_x, width_y)

    def middle(h, arrived, act):
        first = h * part_near
        here = pl.BlockSpec((1, 1) + plane_shape[2:], lambda z: (0, first + z, 0, 0, 0))
        constants = [pointwise_weight, spread, tab["y_fwd"], tab["x_fwd"], tab["y_inv"], tab["x_inv"]]
        operands, in_specs = plane_specs(arrived, 1)
        operands = [*operands, fields, cotangent, *constants]
        in_specs = in_specs + [here, here] + [whole_spec(v) for v in constants]
        body = functools.partial(middle_kernel, groups)
        aliases = {}
        if act is not None:
            aliases = {len(operands): 0, len(operands) + 1: 1}
            operands += act
            in_specs += [pl.BlockSpec(memory_space=pl.ANY)] * 2
            plain = body

            def body(*refs):
                n = len(in_specs)
                plain(*refs[:n - 2], *refs[n:])

        return pl.pallas_call(
            body,
            grid=(part_near,),
            in_specs=in_specs,
            out_specs=[here, pl.BlockSpec((1,) + scratch_planes, lambda z: (first + z, 0, 0, 0)),
                       pl.BlockSpec((channels, channels), lambda z: (0, 0))] + [block(1)] * chips,
            out_shape=[jax.ShapeDtypeStruct(fields.shape, BF16),
                       jax.ShapeDtypeStruct((near, *scratch_planes), F32),
                       jax.ShapeDtypeStruct((channels, channels), F32)] + sent(part_near),
            scratch_shapes=[*scratch(1), pltpu.VMEM((1, *scratch_planes), F32),
                            pltpu.VMEM((1, *scratch_planes), BF16),
                            pltpu.VMEM((1, *scratch_planes), BF16),
                            pltpu.VMEM((side, side), BF16), pltpu.VMEM((side, side), BF16),
                            pltpu.VMEM((side, side), F32)],
            input_output_aliases=aliases,
            compiler_params=params(1),
            name="middle%d" % h,
            cost_estimate=cost(18),
        )(*operands)

    act, points, arrived = None, [], []
    for h in range(cut_out):
        if h:
            point, values = lax.optimization_barrier((points[-1], [v for v, _ in planes[h]]))
            points[-1] = point
            planes[h] = [(v, lead) for v, (_, lead) in zip(values, planes[h])]
        layer_output, part, point, *blocks = middle(h, planes[h], act)
        act = [layer_output, part]
        points.append(point)
        if h:
            blocks, crossed = lax.optimization_barrier((blocks, crossed))
        else:
            crossed = cross(blocks)
        if h:
            arrived = [swap(crossed)]
            crossed = cross(blocks)
            point = sum(points).reshape(-1, QUAD * M)
            k = 1
            while k < groups:
                point = point + hop(point, k)
                k *= 2
            crossed[0], point = lax.optimization_barrier((crossed[0], point))
            arrived.append(swap(crossed))

    last = arrived[-1][1][0]
    last, u_all = lax.optimization_barrier((last, u_all))
    arrived[-1] = [(last if j % CORES else v, lead) for j, (v, lead) in enumerate(arrived[-1])]

    dv_spec, adjoint = mix_call(adjoint_kernel, "mix_adjoint", arrived, (False,), scale, point)
    crossed = cross(adjoint[0])
    dv_all = gather(dv_spec)
    planes = swap(crossed)
    operands, in_specs = plane_specs(planes, batch)
    point = sum(v[0, channels, :point.shape[0]] for v in dv_all).reshape(channels, channels)
    pointwise_grad = point * (1.0 / math.sqrt(cells))

    input_grad = pl.pallas_call(
        functools.partial(final_kernel, groups),
        grid=(near // batch,),
        in_specs=in_specs + [pl.BlockSpec((batch,) + scratch_planes, lambda z: (z, 0, 0, 0)),
                             whole_spec(tab["y_inv"]), whole_spec(tab["x_inv"])],
        out_specs=plane,
        out_shape=jax.ShapeDtypeStruct(fields.shape, BF16),
        scratch_shapes=scratch(batch),
        compiler_params=params(1),
        name="input_gradient",
        cost_estimate=cost(10),
    )(*operands, part, tab["y_inv"], tab["x_inv"])

    tall = 8
    spec_block = pl.BlockSpec((2, channels + 1, tall, QUAD * M), lambda q: (0, 0, q, 0))
    spectral_grad = pl.pallas_call(
        functools.partial(weight_grad_kernel, math.sqrt(total_modes / cells)),
        grid=(places // tall,),
        in_specs=[pl.BlockSpec((samples, 2, channels, tall, QUAD * M), lambda q: (0, 0, 0, q, 0))]
        + [spec_block] * samples,
        out_specs=pl.BlockSpec((2, channels, channels, tall * QUAD * M), lambda q: (0, 0, 0, q)),
        out_shape=jax.ShapeDtypeStruct(spectral_weight.shape, F32),
        compiler_params=params(1),
        name="weight_gradient",
        cost_estimate=cost(9),
    )(u_all, *dv_all)

    return layer_output, input_grad, pointwise_grad, spectral_grad


def solution(mesh):
    placed = (
        P("dp", "gz", None, None, None),
        P("dp", "gz", None, None, None),
        P(None, None, None, "gz"),
        P(),
    )
    return jax.shard_map(
        shards,
        mesh=mesh,
        in_specs=placed,
        out_specs=(
            P("dp", "gz", None, None, None),
            P("dp", "gz", None, None, None),
            P(),
            P(None, None, None, "gz"),
        ),
        check_vma=False,
    )
```

```python
import functools
import math

import jax
import jax.numpy as jnp
import ml_dtypes
import numpy as np
from jax import lax
from jax.experimental import pallas as pl
from jax.experimental.pallas import tpu as pltpu
from jax.sharding import PartitionSpec as P

M = 32
QUAD = 4
CORES = 2
GROUP = 16
F32 = jnp.float32
BF16 = jnp.bfloat16
NN = (((1,), (0,)), ((), ()))
TN = (((0,), (0,)), ((), ()))
NT = (((1,), (1,)), ((), ()))
GELU_A = math.sqrt(2.0 / math.pi)
GELU_B = 0.044715


def halves(table):
    high = table.astype(np.float32).astype(ml_dtypes.bfloat16)
    low = (table - high.astype(np.float64)).astype(np.float32).astype(ml_dtypes.bfloat16)
    return high, low


def thrice(table):
    high, low = halves(table)
    return np.concatenate([high, low, high])


def trig(length, modes):
    phase = np.outer(np.arange(length), modes) % length
    angles = phase * (2.0 * math.pi / length)
    return np.cos(angles), np.sin(angles)


def complex_block(cos, sin, sign):
    return np.array([[cos, sign * sin], [-sign * sin, cos]])


def tables(width_x, width_y, depth, owned_x):
    order_y = (np.arange(M) % (M // QUAD)) * QUAD + np.arange(M) // (M // QUAD)
    cos_x, sin_x = trig(width_x, np.arange(M))
    cos_y, sin_y = trig(width_y, order_y)
    cos_z, sin_z = trig(depth, np.arange(M))
    eye4 = np.eye(QUAD)
    eye_a = np.eye(owned_x)
    y_fwd = np.einsum("pq,ryb->pyrqb", eye4, np.array([cos_y, -sin_y]))
    y_fwd = y_fwd.reshape(QUAD * width_y, 2 * QUAD * M)
    y_inv = np.einsum("pq,ryb->rpbqy", eye4, np.array([cos_y, -sin_y]))
    y_inv = y_inv.reshape(2 * QUAD * M, QUAD * width_y)
    x_fwd = np.einsum("ijxa->ajix", complex_block(cos_x, sin_x, -1.0)).reshape(2 * M, 2 * width_x)
    x_inv = np.einsum("ijxa->jxai", complex_block(cos_x, sin_x, 1.0)).reshape(2 * width_x, 2 * M)
    ones = np.ones(QUAD)
    z_fwd = np.einsum("ac,ijzk,r->zaicjrk", eye_a, complex_block(cos_z, sin_z, -1.0), ones)
    z_fwd = z_fwd.reshape(depth * owned_x * 2, owned_x * 2 * QUAD * M)
    z_inv = np.einsum("ac,ijzk,r->zcjairk", eye_a, complex_block(cos_z, sin_z, 1.0), ones)
    z_inv = z_inv.reshape(depth * owned_x * 2, owned_x * 2 * QUAD * M)
    xi_h, xi_l = halves(x_inv)
    x_inv4 = np.concatenate([xi_h, xi_l, xi_h, xi_l], axis=1)
    x_fwd2 = np.concatenate(halves(x_fwd), axis=0)
    return dict(
        y_fwd=thrice(y_fwd),
        y_inv=thrice(y_inv),
        x_fwd=x_fwd2,
        x_inv=x_inv4,
        z_fwd=np.stack(halves(z_fwd)),
        z_inv=np.stack(halves(z_inv)),
    )


def split(values):
    high = values.astype(BF16)
    return high, (values - high.astype(F32)).astype(BF16)


def dot(left, right, dims=NN):
    return lax.dot_general(left, right, dims, preferred_element_type=F32)


def x_forward(real, imag, x_fwd_ref):
    high, low = split(jnp.concatenate([real, imag], axis=0))
    both = dot(x_fwd_ref[...], high)
    rows = both.shape[0] // 2
    return both[:rows] + both[rows:] + dot(x_fwd_ref[:rows], low)


def slot(j, h, chips, first):
    c, k = j // CORES, j % CORES
    base = sum(chips + f for f in first[:h])
    if not first[h]:
        return base + c, k
    return (base + c, 0) if k == 0 else (base + chips, c)


def store_blocks(out_refs, scratch, values, me, t):
    groups, rows = scratch.shape[:2]
    for d in range(groups):
        scratch[d] = values[d * rows:(d + 1) * rows]
    for j in range(groups):
        i, lead = slot(j, 0, groups // CORES, (False,))
        out_refs[i][lead, t] = scratch[me ^ j]


def load_blocks(in_refs, scratch, flat, me, t):
    groups, rows = scratch.shape[:2]
    for j, ref in enumerate(in_refs):
        scratch[me ^ j] = ref[0, t]
    if rows % 8 == 0:
        return scratch[...].reshape(groups * rows, scratch.shape[2])
    for d in range(groups):
        flat[d * rows:(d + 1) * rows] = scratch[d]
    return flat[...]


def fields_kernel(f_ref, y_fwd_ref, x_fwd_ref, *refs):
    out_refs, v_scr = refs[:-1], refs[-1]
    channels = f_ref.shape[2]
    for t in range(f_ref.shape[1]):
        real, imag = [], []
        for j in range(channels // QUAD):
            planes = [f_ref[0, t, QUAD * j + p] for p in range(QUAD)]
            g = dot(jnp.concatenate(planes + planes, axis=1), y_fwd_ref[:2 * QUAD * f_ref.shape[4]])
            half = g.shape[1] // 2
            real.append(g[:, :half])
            imag.append(g[:, half:])
        values = x_forward(jnp.concatenate(real, axis=1), jnp.concatenate(imag, axis=1), x_fwd_ref)
        store_blocks(out_refs, v_scr.at[t], values, lax.axis_index("gz"), t)


def inverse_planes(p, x_inv_ref, y_inv_ref):
    high, low = split(p)
    q = dot(x_inv_ref[...], jnp.concatenate([high, high, low, low], axis=0))
    q_high, q_low = split(q)
    rows = q.shape[0] // 2
    wide = QUAD * M
    for j in range(q.shape[1] // wide):
        here = slice(j * wide, (j + 1) * wide)
        high = [q_high[:rows, here], q_high[rows:, here]]
        low = [q_low[:rows, here], q_low[rows:, here]]
        yield j, dot(jnp.concatenate(high + high + low, axis=1), y_inv_ref[...])


def middle_kernel(groups, *refs):
    in_refs, inputs, (act_ref, part_ref, pg_ref), out_refs, scratch = cut(
        refs, groups, 8, 3, groups // CORES, 8)
    f_ref, cot_ref, w_ref, spread_ref, y_fwd_ref, x_fwd_ref, y_inv_ref, x_inv_ref = inputs
    p_scr, flat, spec, g_high, g_low, w1_ref, w2_ref, pg_scr = scratch
    me = lax.axis_index("gz")
    channels, width_x, width_y = f_ref.shape[2:]
    group = GROUP
    side = channels * group
    same = (lax.broadcasted_iota(jnp.int32, (side, side), 0) % group
            == lax.broadcasted_iota(jnp.int32, (side, side), 1) % group)

    @pl.when(pl.program_id(0) == 0)
    def _():
        pg_scr[...] = jnp.zeros_like(pg_scr)
        spread = spread_ref[...]
        for ref, dims in ((w1_ref, NT), (w2_ref, NN)):
            rows = dot(spread, w_ref[...], dims).astype(BF16)
            ref[...] = jnp.where(same, dot(rows, spread, NT), 0.0).astype(BF16)

    for t in range(f_ref.shape[1]):
        for j, value in inverse_planes(load_blocks(in_refs, p_scr.at[t], flat.at[t], me, t), x_inv_ref, y_inv_ref):
            for p in range(QUAD):
                spec[t, QUAD * j + p] = value[:, p * width_y:(p + 1) * width_y]

        rows = channels * group

        def step(u, carry):
            first = pl.multiple_of(u * 2 * group, 2 * group)
            cells = [pl.ds(first, group), pl.ds(first + group, group)]

            def both(read):
                return jnp.concatenate([read(s).reshape(rows, width_y) for s in cells], axis=1)

            f = both(lambda s: f_ref[0, t, :, s, :])
            pre = dot(w1_ref[...], f) + both(lambda s: spec[t, :, s, :])
            square = pre * pre
            t_val = jnp.tanh(GELU_A * pre * (1.0 + GELU_B * square))
            cdf = 0.5 + 0.5 * t_val
            act = (pre * cdf).astype(BF16)
            slope = cdf + pre * (0.5 - 0.5 * t_val * t_val) * (GELU_A + 3.0 * GELU_A * GELU_B * square)
            g = both(lambda s: cot_ref[0, t, :, s, :]).astype(F32) * slope
            high, low = split(g)
            part = dot(w2_ref[...], high) + dot(w2_ref[...], low)
            pg = None
            for i, s in enumerate(cells):
                lanes = slice(i * width_y, (i + 1) * width_y)
                shape = (channels, group, width_y)
                act_ref[0, t, :, s, :] = act[:, lanes].reshape(shape)
                part_ref[t, :, s, :] = part[:, lanes].reshape(shape)
                g_high[t, :, s, :] = high[:, lanes].reshape(shape)
                g_low[t, :, s, :] = low[:, lanes].reshape(shape)
            pg_scr[...] += dot(f, high, NT) + dot(f, low, NT)
            return carry

        lax.fori_loop(0, width_x // (2 * group), step, 0, unroll=True)

        real, imag = [], []
        for j in range(channels // QUAD):
            high, low = [[r[t, QUAD * j + p] for p in range(QUAD)] for r in (g_high, g_low)]
            v = dot(jnp.concatenate(high + high + low, axis=1), y_fwd_ref[...])
            half = v.shape[1] // 2
            real.append(v[:, :half])
            imag.append(v[:, half:])
        values = x_forward(jnp.concatenate(real, axis=1), jnp.concatenate(imag, axis=1), x_fwd_ref)
        store_blocks(out_refs, p_scr.at[t], values, me, t)

    @pl.when(pl.program_id(0) == pl.num_programs(0) - 1)
    def _():
        spread = spread_ref[...].astype(F32)
        kept = jnp.where(same, pg_scr[...], 0.0)
        right = lax.dot_general(kept, spread, NN, precision=lax.Precision.HIGHEST, preferred_element_type=F32)
        pg_ref[...] = lax.dot_general(spread, right, TN, precision=lax.Precision.HIGHEST, preferred_element_type=F32)


def final_kernel(groups, *refs):
    in_refs, (part_ref, y_inv_ref, x_inv_ref, out_ref, p_scr, flat) = cut(refs, groups, 6)
    me = lax.axis_index("gz")
    width_y = out_ref.shape[4]
    for t in range(out_ref.shape[1]):
        for j, value in inverse_planes(load_blocks(in_refs, p_scr.at[t], flat.at[t], me, t), x_inv_ref, y_inv_ref):
            for p in range(QUAD):
                c = QUAD * j + p
                out_ref[0, t, c] = (value[:, p * width_y:(p + 1) * width_y] + part_ref[t, c]).astype(BF16)


def lane_quad(shape):
    return lax.broadcasted_iota(jnp.int32, shape, len(shape) - 1) // M


def depth_forward(in_refs, s_scr, z_fwd_ref, spec_ref, scale):
    me = lax.axis_index("gz")
    groups = s_scr.shape[0]
    tall = s_scr.shape[1] * groups // len(in_refs)
    for i, ref in enumerate(in_refs):
        h, j = i // groups, i % groups
        s_scr[me ^ j, h * tall:(h + 1) * tall] = ref[0]
    high, low = split(s_scr[...].reshape(-1, s_scr.shape[2]))
    v = dot(high, z_fwd_ref[0], TN) + dot(high, z_fwd_ref[1], TN) + dot(low, z_fwd_ref[0], TN)
    tall = M // QUAD
    wide = QUAD * M
    channels = v.shape[0] // M
    v = v.reshape(channels, QUAD, tall, v.shape[1])
    quad = lane_quad((channels, tall, wide))
    for a in range(v.shape[3] // (2 * wide)):
        for part in range(2):
            lanes = slice((2 * a + part) * wide, (2 * a + part + 1) * wide)
            u = v[:, 0, :, lanes]
            for r in range(1, QUAD):
                u = jnp.where(quad == r, v[:, r, :, lanes], u)
            spec_ref[part, :channels, a * tall:(a + 1) * tall, :] = u * scale if scale != 1.0 else u


def depth_inverse(spec_ref, z_inv_ref, s_scr, out_refs, first):
    channels, places, wide = spec_ref.shape[1:]
    tall = M // QUAD
    quad = lane_quad((channels, tall, wide))
    pieces = []
    for a in range(places // tall):
        for part in range(2):
            v = spec_ref[part, :, a * tall:(a + 1) * tall, :]
            masked = jnp.stack([jnp.where(quad == r, v, 0.0) for r in range(QUAD)], axis=1)
            pieces.append(masked.reshape(channels * M, wide))
    high, low = split(jnp.concatenate(pieces, axis=1))
    values = dot(z_inv_ref[0], high, NT) + dot(z_inv_ref[1], high, NT) + dot(z_inv_ref[0], low, NT)
    s_scr[...] = values.reshape(s_scr.shape)
    me = lax.axis_index("gz")
    groups = s_scr.shape[0]
    tall = s_scr.shape[1] // len(first)
    for h in range(len(first)):
        for j in range(groups):
            i, lead = slot(j, h, groups // CORES, first)
            out_refs[i][lead] = s_scr[me ^ j, h * tall:(h + 1) * tall]


def cut(refs, *counts):
    pieces = []
    for n in counts:
        pieces.append(refs[:n])
        refs = refs[n:]
    return pieces


def mix_kernel(count_in, count_out, first, scale, *refs):
    in_refs, (r_ref, z_fwd_ref, z_inv_ref, u_ref), out_refs, (v_scr, s_scr) = cut(refs, count_in, 4, count_out, 2)
    channels, places, wide = u_ref.shape[1:]
    depth_forward(in_refs, s_scr, z_fwd_ref, u_ref, 1.0)

    def step(q, carry):
        lanes = pl.ds(pl.multiple_of(q * wide, wide), wide)
        real = jnp.zeros((channels, wide), F32)
        imag = jnp.zeros((channels, wide), F32)
        for c in range(channels):
            w_re = r_ref[0, c, :, lanes].astype(F32)
            w_im = r_ref[1, c, :, lanes].astype(F32)
            u_re = u_ref[0, c, pl.ds(q, 1), :]
            u_im = u_ref[1, c, pl.ds(q, 1), :]
            real += u_re * w_re - u_im * w_im
            imag += u_re * w_im + u_im * w_re
        v_scr[0, :, pl.ds(q, 1), :] = (real * scale)[:, None, :]
        v_scr[1, :, pl.ds(q, 1), :] = (imag * scale)[:, None, :]
        return carry

    lax.fori_loop(0, places, step, 0)
    depth_inverse(v_scr, z_inv_ref, s_scr, out_refs, first)


def adjoint_kernel(count_in, count_out, first, scale, *refs):
    in_refs, (point_ref, r_ref, z_fwd_ref, z_inv_ref, dv_ref), out_refs, (du_scr, s_scr) = cut(
        refs, count_in, 5, count_out, 2)
    channels, places, wide = du_scr.shape[1:]
    dv_ref[:, channels:] = jnp.zeros((2, 1, places, wide), F32)
    dv_ref[0, channels, 0:point_ref.shape[0]] = point_ref[...]
    depth_forward(in_refs, s_scr, z_fwd_ref, dv_ref, scale)

    def step(q, carry):
        lanes = pl.ds(pl.multiple_of(q * wide, wide), wide)
        d_re = dv_ref[0, :channels, pl.ds(q, 1), :].reshape(channels, wide)
        d_im = dv_ref[1, :channels, pl.ds(q, 1), :].reshape(channels, wide)
        for c in range(channels):
            w_re = r_ref[0, c, :, lanes].astype(F32)
            w_im = r_ref[1, c, :, lanes].astype(F32)
            du_scr[0, c, pl.ds(q, 1), :] = jnp.sum(d_re * w_re + d_im * w_im, axis=0, keepdims=True)
            du_scr[1, c, pl.ds(q, 1), :] = jnp.sum(d_im * w_re - d_re * w_im, axis=0, keepdims=True)
        return carry

    lax.fori_loop(0, places, step, 0)
    depth_inverse(du_scr, z_inv_ref, s_scr, out_refs, first)


def weight_grad_kernel(scale, *refs):
    u_ref, dv_refs, out_ref = refs[0], refs[1:-1], refs[-1]
    count = len(dv_refs)
    me = lax.axis_index("dp")
    channels, places, wide = u_ref.shape[2:]
    for q in range(places):
        lanes = slice(q * wide, (q + 1) * wide)
        dv = [[r[part, :channels, q, :] * scale for part in range(2)] for r in dv_refs]
        for c in range(channels):
            real = imag = None
            for s in range(count):
                u_re = u_ref[me ^ s, 0, c, q:q + 1, :]
                u_im = u_ref[me ^ s, 1, c, q:q + 1, :]
                d_re, d_im = dv[s]
                t_re = u_re * d_re + u_im * d_im
                t_im = u_re * d_im - u_im * d_re
                real = t_re if real is None else real + t_re
                imag = t_im if imag is None else imag + t_im
            out_ref[0, c, :, lanes] = real
            out_ref[1, c, :, lanes] = imag


def params(steps, megabytes=24):
    return pltpu.CompilerParams(
        dimension_semantics=("arbitrary",) * steps, vmem_limit_bytes=megabytes * 1024 * 1024
    )


def cost(micros):
    return pl.CostEstimate(flops=int(micros * 1.1e9), bytes_accessed=int(micros * 3.5e6), transcendentals=0)


def whole_spec(array):
    rank = len(array.shape)
    return pl.BlockSpec(tuple(array.shape), lambda *i: (0,) * rank)


def shards(fields, cotangent, spectral_weight, pointwise_weight):
    groups = lax.axis_size("gz")
    samples = lax.axis_size("dp")
    _, near, channels, width_x, width_y = fields.shape
    depth = near * groups
    owned = M // groups
    rows = 2 * owned
    wide = channels * M
    places = spectral_weight.shape[3] // (QUAD * M)
    total_modes = M * M * M
    cells = samples * width_x * width_y * depth
    scale = 1.0 / math.sqrt(width_x * width_y * depth * total_modes)
    tab = {k: jnp.asarray(v) for k, v in tables(width_x, width_y, depth, owned).items()}

    chips = groups // CORES
    cut_out = 2
    part_near = near // cut_out
    batch = 2
    plane_shape = (1, batch, channels, width_x, width_y)
    plane = pl.BlockSpec(plane_shape, lambda z: (0, z, 0, 0, 0))

    def block(planes):
        return pl.BlockSpec((CORES, planes, rows, wide), lambda z: (0, z, 0, 0))

    def scratch(planes):
        return [pltpu.VMEM((planes, groups, rows, wide), F32),
                pltpu.VMEM((planes, groups * rows if rows % 8 else 8, wide), F32)]

    spec_shape = jax.ShapeDtypeStruct((2, channels, places, QUAD * M), F32)

    def sent(planes):
        return [jax.ShapeDtypeStruct((CORES, planes, rows, wide), F32)] * chips

    def hop(values, j):
        return lax.ppermute(values, "gz", [(i, i ^ j) for i in range(groups)])

    far_first = sorted(range(1, chips), key=lambda c: (-(c & (chips // 2)), c))

    def cross(blocks):
        got = [blocks[0]] + [None] * (chips - 1)
        for c in far_first:
            got[c] = hop(blocks[c], CORES * c)
        return got

    def swap(got):
        swapped = hop(jnp.stack([g[1] for g in got]), 1)
        return [(got[j // CORES], 0) if j % CORES == 0 else (swapped, j // CORES) for j in range(groups)]

    def swap_last(blocks):
        return swap(cross(blocks))

    def swap_first(blocks):
        *near_blocks, crossing = blocks
        swapped = hop(crossing, 1)
        got = [None] * chips
        for c in far_first:
            got[c] = hop(jnp.concatenate([near_blocks[c], swapped[c:c + 1]]), CORES * c)
        return [(near_blocks[0], 0), (swapped, 0)] + [(got[j // CORES], j % CORES) for j in range(CORES, groups)]

    def reshaped(arrays, *shape):
        return [v.reshape(v.shape[0], *shape) for v in arrays]

    def gather(values):
        pieces = [values]
        for k in range(1, samples):
            pieces.append(lax.ppermute(values, "dp", [(i, i ^ k) for i in range(samples)]))
        return pieces

    def plane_specs(arrived, planes):
        def one(lead):
            return pl.BlockSpec((1, planes, rows, wide), lambda z: (lead, z, 0, 0))
        return [v for v, _ in arrived], [one(lead) for _, lead in arrived]

    def mix_call(kernel, name, arrived, first, factor, *extra):
        pieces = [p for half in arrived for p in half]
        tall = near // len(arrived) * rows
        operands = [v.reshape(v.shape[0], tall, wide) for v, _ in pieces]

        def one(lead):
            return pl.BlockSpec((1, tall, wide), lambda i: (lead, 0, 0))

        constants = [*extra, spectral_weight, tab["z_fwd"], tab["z_inv"]]
        made = jax.ShapeDtypeStruct((2, channels + len(extra), places, QUAD * M), F32)
        halves = len(first)
        low = near // halves * rows
        outs = []
        for f in first:
            outs += [jax.ShapeDtypeStruct((1 if f else CORES, low, wide), F32)] * chips
            outs += [jax.ShapeDtypeStruct((chips, low, wide), F32)] * f
        result = pl.pallas_call(
            functools.partial(kernel, len(operands), len(outs), first, factor),
            grid=(1,),
            in_specs=[one(lead) for _, lead in pieces] + [whole_spec(v) for v in constants],
            out_specs=[whole_spec(made)] + [whole_spec(v) for v in outs],
            out_shape=[made] + outs,
            scratch_shapes=[pltpu.VMEM(spec_shape.shape, F32), pltpu.VMEM((groups, near * rows, wide), F32)],
            compiler_params=params(1, 24),
            name=name,
            cost_estimate=cost(9),
        )(*operands, *constants)
        blocks = reshaped(result[1:], near // halves, rows, wide)
        return result[0], cut(blocks, *[chips + f for f in first])

    forward = pl.pallas_call(
        fields_kernel,
        grid=(near // batch,),
        in_specs=[plane, whole_spec(tab["y_fwd"]), whole_spec(tab["x_fwd"])],
        out_specs=[block(batch)] * chips,
        out_shape=sent(near),
        scratch_shapes=scratch(batch)[:1],
        compiler_params=params(1),
        name="fields_forward",
        cost_estimate=cost(5),
    )(fields, tab["y_fwd"], tab["x_fwd"])
    arrived = [swap_last(forward)]

    u_spec, mixed = mix_call(mix_kernel, "mix_modes", arrived, (False,) * cut_out, scale)
    planes = [cross(m) for m in mixed]
    u_all = lax.all_gather(u_spec, "dp")

    side = channels * GROUP
    spread = jnp.asarray(np.kron(np.eye(channels), np.ones((GROUP, 1))).astype(ml_dtypes.bfloat16))
    scratch_planes = (channels, width_x, width_y)

    def middle(h, arrived, act):
        first = h * part_near
        here = pl.BlockSpec((1, 1) + plane_shape[2:], lambda z: (0, first + z, 0, 0, 0))
        constants = [pointwise_weight, spread, tab["y_fwd"], tab["x_fwd"], tab["y_inv"], tab["x_inv"]]
        operands, in_specs = plane_specs(arrived, 1)
        operands = [*operands, fields, cotangent, *constants]
        in_specs = in_specs + [here, here] + [whole_spec(v) for v in constants]
        body = functools.partial(middle_kernel, groups)
        aliases = {}
        if act is not None:
            aliases = {len(operands): 0, len(operands) + 1: 1}
            operands += act
            in_specs += [pl.BlockSpec(memory_space=pl.ANY)] * 2
            plain = body

            def body(*refs):
                n = len(in_specs)
                plain(*refs[:n - 2], *refs[n:])

        return pl.pallas_call(
            body,
            grid=(part_near,),
            in_specs=in_specs,
            out_specs=[here, pl.BlockSpec((1,) + scratch_planes, lambda z: (first + z, 0, 0, 0)),
                       pl.BlockSpec((channels, channels), lambda z: (0, 0))] + [block(1)] * chips,
            out_shape=[jax.ShapeDtypeStruct(fields.shape, BF16),
                       jax.ShapeDtypeStruct((near, *scratch_planes), F32),
                       jax.ShapeDtypeStruct((channels, channels), F32)] + sent(part_near),
            scratch_shapes=[*scratch(1), pltpu.VMEM((1, *scratch_planes), F32),
                            pltpu.VMEM((1, *scratch_planes), BF16),
                            pltpu.VMEM((1, *scratch_planes), BF16),
                            pltpu.VMEM((side, side), BF16), pltpu.VMEM((side, side), BF16),
                            pltpu.VMEM((side, side), F32)],
            input_output_aliases=aliases,
            compiler_params=params(1),
            name="middle%d" % h,
            cost_estimate=cost(18),
        )(*operands)

    act, points, arrived = None, [], []
    for h in range(cut_out):
        if h:
            points[-1], planes[h] = lax.optimization_barrier((points[-1], planes[h]))
        layer_output, part, point, *blocks = middle(h, swap(planes[h]), act)
        act = [layer_output, part]
        points.append(point)
        if h:
            blocks, crossed = lax.optimization_barrier((blocks, crossed))
        else:
            crossed = cross(blocks)
        if h:
            arrived = [swap(crossed)]
            crossed = cross(blocks)
            point = sum(points).reshape(-1, QUAD * M)
            k = 1
            while k < groups:
                point = point + hop(point, k)
                k *= 2
            crossed[0], point = lax.optimization_barrier((crossed[0], point))
            arrived.append(swap(crossed))

    last = arrived[-1][1][0]
    last, u_all = lax.optimization_barrier((last, u_all))
    arrived[-1] = [(last if j % CORES else v, lead) for j, (v, lead) in enumerate(arrived[-1])]

    dv_spec, adjoint = mix_call(adjoint_kernel, "mix_adjoint", arrived, (False,), scale, point)
    crossed = cross(adjoint[0])
    dv_all = gather(dv_spec)
    planes = swap(crossed)
    operands, in_specs = plane_specs(planes, batch)
    point = sum(v[0, channels, :point.shape[0]] for v in dv_all).reshape(channels, channels)
    pointwise_grad = point * (1.0 / math.sqrt(cells))

    input_grad = pl.pallas_call(
        functools.partial(final_kernel, groups),
        grid=(near // batch,),
        in_specs=in_specs + [pl.BlockSpec((batch,) + scratch_planes, lambda z: (z, 0, 0, 0)),
                             whole_spec(tab["y_inv"]), whole_spec(tab["x_inv"])],
        out_specs=plane,
        out_shape=jax.ShapeDtypeStruct(fields.shape, BF16),
        scratch_shapes=scratch(batch),
        compiler_params=params(1),
        name="input_gradient",
        cost_estimate=cost(10),
    )(*operands, part, tab["y_inv"], tab["x_inv"])

    tall = 8
    spec_block = pl.BlockSpec((2, channels + 1, tall, QUAD * M), lambda q: (0, 0, q, 0))
    spectral_grad = pl.pallas_call(
        functools.partial(weight_grad_kernel, math.sqrt(total_modes / cells)),
        grid=(places // tall,),
        in_specs=[pl.BlockSpec((samples, 2, channels, tall, QUAD * M), lambda q: (0, 0, 0, q, 0))]
        + [spec_block] * samples,
        out_specs=pl.BlockSpec((2, channels, channels, tall * QUAD * M), lambda q: (0, 0, 0, q)),
        out_shape=jax.ShapeDtypeStruct(spectral_weight.shape, F32),
        compiler_params=params(1),
        name="weight_gradient",
        cost_estimate=cost(9),
    )(u_all, *dv_all)

    return layer_output, input_grad, pointwise_grad, spectral_grad


def solution(mesh):
    placed = (
        P("dp", "gz", None, None, None),
        P("dp", "gz", None, None, None),
        P(None, None, None, "gz"),
        P(),
    )
    return jax.shard_map(
        shards,
        mesh=mesh,
        in_specs=placed,
        out_specs=(
            P("dp", "gz", None, None, None),
            P("dp", "gz", None, None, None),
            P(),
            P(None, None, None, "gz"),
        ),
        check_vma=False,
    )
```
